32 devices in a mesh: half: 2 (over core), row: 4 (over z), col: 4 (over y, x).
Axes of the slice: x: 2, y: 2, z: 4, core: 2. Of those that a mesh axis runs over, the one named last changes fastest.
Arguments:
- samples: bfloat16 [16384, 512], P(('half', 'row'), 'col'), may hold values from -6 to 6
- couplings: bfloat16 [256, 64, 512], P(('half', 'row')), may hold values from -0.25 to 0.25
- coupling_cols: int32 [256, 8], P(('half', 'row')), may hold values from 0 to 255, as said below
- child_map: int32 [2, 4, 64], P('half', 'row'), may hold values from 0 to 63, each once within a row
- gen_left: bfloat16 [2, 256, 16384], P('half', 'col', 'row'), may hold values from -0.375 to 0.375
- gen_right: bfloat16 [2, 256, 16384], P('half', 'col', 'row'), may hold values from -0.046875 to 0.046875
Outputs:
- range_samples: bfloat16 [16384, 512], P(('half', 'row'), 'col')
- row_samples: bfloat16 [16384, 512], P(('half', 'row'), 'col')
The draws below stay inside these ranges and needn't reach their ends.
Inputs may be any that keep to these rules, and one draw needn't show every extreme that they name: `coupling_cols`: slot 0 of block row b is b itself, and every entry lies within 8 blocks of its block row. `child_map`: for each child and row group, the last dimension is a permutation.
All inputs are finite; a program needn't handle non-finite values.
Results may differ from the reference program's by a relative error of at most 0.0075.
Values may be sent and summed in bfloat16 or wider, within the bound.
A program may use at most 64 MiB of HBM per device.

```python
import jax
import jax.numpy as jnp
from jax import lax

BS = 64
NB = 8
HB = 8
S = 512
K = 256
BLK_DEV = 32
GROUPS = 4
NBK = 256
NF = 16384
N_HALF = 2
N_ROW = 4


def draw_coupling_cols(key, part):
    block_rows = jnp.arange(NBK, dtype=jnp.int32)[:, None]
    offsets = jax.random.randint(key, (NBK, NB), -HB, HB + 1, dtype=jnp.int32)
    offsets = offsets.at[:, 0].set(0)
    return jnp.clip(block_rows + offsets, 0, NBK - 1).astype(jnp.int32)


def steps_of(rng, extent, split, least, largest):
    factor_of, own = 1.0, jax.random.fold_in(rng, 6)
    for dim, parts in split:
        heights = jnp.exp(jax.random.uniform(jax.random.fold_in(own, dim), (parts,), jnp.float32, least / len(split), largest / len(split)))
        factor_of = factor_of * jnp.repeat(heights, extent[dim] // parts).reshape([-1 if axis == dim else 1 for axis in range(len(extent))])
    return factor_of


def scatter_about(stream_key, dims, scale, reach, split=(), held_as=jnp.bfloat16):
    drawn = scale * jax.random.normal(stream_key, dims, jnp.float32)
    if split:
        drawn = drawn * steps_of(stream_key, dims, split, -0.22, 0.18)
    return jnp.clip(drawn, -reach, reach).astype(held_as)


def setup_inputs(seed: int = 0) -> dict:
    arg_keys = jax.random.split(jax.random.key(seed), 7)
    samples = scatter_about(arg_keys[0], (NF, S), 1.0, 6.0, ((0, 8), (1, 4)))
    couplings = scatter_about(arg_keys[1], (NBK, BS, NB * BS), (NB * BS) ** -0.5, 0.25, ((0, 8),))
    coupling_cols = draw_coupling_cols(jax.random.fold_in(arg_keys[6], 71), 0)
    child_map = jax.vmap(lambda own: jax.random.permutation(own, 2 * BLK_DEV))(jax.random.split(arg_keys[3], N_HALF * GROUPS)).reshape((N_HALF, GROUPS, 2 * BLK_DEV)).astype(jnp.int32)
    gen_left = scatter_about(arg_keys[4], (N_HALF, K, NF), K ** -0.5, 0.375, ((0, 2), (1, 4), (2, 4)))
    gen_right = scatter_about(arg_keys[5], (N_HALF, K, NF), NF ** -0.5, 0.046875, ((0, 2), (1, 4), (2, 4)))
    return dict(samples=samples, couplings=couplings, coupling_cols=coupling_cols, child_map=child_map, gen_left=gen_left, gen_right=gen_right)


def front_index(order_map):
    piece = 2 * BLK_DEV // N_ROW
    source = order_map // piece
    within = order_map % piece
    slot = jnp.arange(N_ROW, dtype=jnp.int32)[:, None] * piece + within
    half_index = slot // BLK_DEV
    return ((half_index * N_ROW + source) * BLK_DEV + slot % BLK_DEV).reshape(-1).astype(jnp.int32)


def reference(samples, couplings, coupling_cols, child_map, gen_left, gen_right):
    total_blocks = NF // BS
    sample_blocks = samples.reshape(total_blocks, BS, S)
    coupling_groups = couplings.reshape(-1, BLK_DEV, BS, NB * BS)
    col_groups = coupling_cols.reshape(-1, BLK_DEV, NB)
    row_groups = sample_blocks.reshape(-1, BLK_DEV, BS, S)

    def range_group(pair):
        block_rows, block_cols = pair
        gathered = sample_blocks[block_cols].reshape(BLK_DEV, NB * BS, S)
        return jnp.einsum('bik,bks->bis', block_rows.astype(jnp.float32), gathered.astype(jnp.float32))

    sparse_range = lax.map(range_group, (coupling_groups, col_groups)).reshape(NF, S)

    def row_group(total, triple):
        block_rows, block_cols, own_rows = triple
        terms = jnp.einsum('bik,bis->bks', block_rows.astype(jnp.float32), own_rows.astype(jnp.float32))
        terms = terms.reshape(BLK_DEV * NB, BS, S)
        return total.at[block_cols.reshape(-1)].add(terms), None

    sparse_rows, unused = lax.scan(row_group, jnp.zeros((total_blocks, BS, S), jnp.float32),
                                   (coupling_groups, col_groups, row_groups))
    child_range = jnp.zeros((total_blocks, BS, S), jnp.float32)
    child_rows = jnp.zeros((total_blocks, BS, S), jnp.float32)
    for child in range(N_HALF):
        mapping = front_index(child_map[child])
        gathered = sample_blocks[mapping].reshape(NF, S)
        left_gen = gen_left[child]
        right_gen = gen_right[child]
        w_block = jnp.dot(right_gen, gathered, preferred_element_type=jnp.float32).astype(jnp.bfloat16)
        g_block = jnp.dot(left_gen, gathered, preferred_element_type=jnp.float32).astype(jnp.bfloat16)
        range_part = jnp.dot(left_gen.T, w_block, preferred_element_type=jnp.float32).astype(jnp.bfloat16)
        rows_part = jnp.dot(right_gen.T, g_block, preferred_element_type=jnp.float32).astype(jnp.bfloat16)
        range_part = lax.optimization_barrier(range_part).astype(jnp.float32)
        rows_part = lax.optimization_barrier(rows_part).astype(jnp.float32)
        child_range = child_range.at[mapping].add(range_part.reshape(total_blocks, BS, S))
        child_rows = child_rows.at[mapping].add(rows_part.reshape(total_blocks, BS, S))
    range_samples = (sparse_range + child_range.reshape(NF, S)).astype(jnp.bfloat16)
    row_samples = (sparse_rows.reshape(NF, S) + child_rows.reshape(NF, S)).astype(jnp.bfloat16)
    return (range_samples, row_samples)
```

```python
import functools

import jax
import jax.numpy as jnp
from jax import lax
from jax.experimental import pallas as pl
from jax.experimental.pallas import tpu as pltpu
from jax.sharding import PartitionSpec as P

BS = 64
NB = 8
HB = 8
MESH = pl.DeviceIdType.MESH
VMEM_LIMIT = 48 * 1024 * 1024
F32 = jnp.float32
BF16 = jnp.bfloat16


def vmem():
    return pl.BlockSpec(memory_space=pltpu.VMEM)


def smem():
    return pl.BlockSpec(memory_space=pltpu.SMEM)


def prepare_kernel(map_ref, left_ref, right_ref, out_ref):
    pairs = left_ref.shape[2] // (2 * BS)

    def step(i, carry):
        lanes = pl.ds(pl.multiple_of(i * 2 * BS, 2 * BS), 2 * BS)
        tile = jnp.concatenate([left_ref[0, :, lanes], right_ref[0, :, lanes]], axis=0).T
        for u in range(2):
            place = pl.multiple_of(map_ref[0, 0, 2 * i + u] * BS, BS)
            out_ref[pl.ds(place, BS), :] = tile[u * BS : (u + 1) * BS]
        return carry

    lax.fori_loop(0, pairs, step, 0, unroll=4)


def sparse_kernel(
    cols_ref, low_ref, x_ref, high_ref, a_ref, range_ref, rows_ref, edge_ref, padded, spread
):
    count = a_ref.shape[0]
    rows = x_ref.shape[0]
    halo = HB * BS
    first = (lax.axis_index("half") * lax.axis_size("row") + lax.axis_index("row")) * count
    padded[:halo] = low_ref[...]
    padded[halo : halo + rows] = x_ref[...]
    padded[halo + rows :] = high_ref[...]
    spread[...] = jnp.zeros_like(spread)

    def step(b, carry):
        at = [
            pl.multiple_of((cols_ref[b, t] - first + HB) * BS, BS) for t in range(NB)
        ]
        a = a_ref[b]
        own = pl.ds(pl.multiple_of(b * BS, BS), BS)
        picked = jnp.concatenate([padded[pl.ds(p, BS), :] for p in at], axis=0)
        range_ref[own, :] = jnp.dot(a, picked, preferred_element_type=F32)
        pieces = lax.dot_general(
            a, x_ref[own, :], (((0,), (0,)), ((), ())), preferred_element_type=F32
        )
        for t in range(NB):
            spread[pl.ds(at[t], BS), :] += pieces[t * BS : (t + 1) * BS]
        return carry

    lax.fori_loop(0, count, step, 0, unroll=2)
    rows_ref[...] = spread[halo : halo + rows]
    edge_ref[0] = spread[:halo].astype(BF16)
    edge_ref[1] = spread[halo + rows :].astype(BF16)


def exchange_kernel(
    n_half,
    n_row,
    n_col,
    gen_ref,
    x_ref,
    range_ref,
    rows_ref,
    edge_ref,
    range_out,
    rows_out,
    gens,
    pair,
    part,
    terms,
    held,
    weights,
    leaving,
    landed,
    halo,
    x_sem,
    z_send,
    z_recv,
    c_send,
    c_recv,
    p_send,
    p_recv,
    q_send,
    q_recv,
    h_send,
    h_recv,
    e_send,
    e_recv,
):
    half, row, col = lax.axis_index("half"), lax.axis_index("row"), lax.axis_index("col")
    rows, panel = x_ref.shape
    total = gen_ref.shape[0]
    chunk = total // n_row
    cut = chunk // 2
    unit = n_col * panel // n_row
    edge = HB * BS
    flat = half * n_row + row
    other = 1 - half
    side_a = col + 1 - 2 * lax.rem(col, 2)
    side_b = lax.rem(col + 2, n_col)

    def ahead(k):
        return lax.rem(row + k, n_row)

    def behind(k):
        return lax.rem(row + n_row - k, n_row)

    def device(index):
        return (index // n_row, lax.rem(index, n_row), col)

    seam_low = jnp.logical_and(half == 0, row == n_row - 1)
    seam_high = jnp.logical_and(half == 1, row == 0)

    barrier = pltpu.get_barrier_semaphore()

    def greet(k, carry):
        pl.semaphore_signal(
            barrier, inc=1, device_id=(half, ahead(k), col), device_id_type=MESH
        )
        return carry

    lax.fori_loop(1, n_row, greet, 0)
    for peer in ((other, row, col), (half, row, side_a), (half, row, side_b)):
        pl.semaphore_signal(barrier, inc=1, device_id=peer, device_id_type=MESH)

    @pl.when(seam_low)
    def _():
        pl.semaphore_signal(
            barrier, inc=1, device_id=(other, ahead(1), col), device_id_type=MESH
        )

    @pl.when(seam_high)
    def _():
        pl.semaphore_signal(
            barrier, inc=1, device_id=(other, behind(1), col), device_id_type=MESH
        )

    seams = jnp.where(jnp.logical_or(seam_low, seam_high), 1, 0)
    pl.semaphore_wait(barrier, n_row + 2 + seams)

    def rows_of(start, size):
        return pl.ds(pl.multiple_of(start, size), size)

    def z_copy(k):
        return pltpu.make_async_remote_copy(
            src_ref=gen_ref.at[rows_of(ahead(k) * chunk, chunk), :],
            dst_ref=gens.at[col, rows_of(row * chunk, chunk), :],
            send_sem=z_send.at[k],
            recv_sem=z_recv.at[k],
            device_id=(half, ahead(k), col),
            device_id_type=MESH,
        )

    def z_arrived(k):
        place = gens.at[col, rows_of(behind(k) * chunk, chunk), :]
        return pltpu.make_async_remote_copy(
            src_ref=place,
            dst_ref=place,
            send_sem=z_send.at[k],
            recv_sem=z_recv.at[k],
            device_id=(half, behind(k), col),
            device_id_type=MESH,
        )

    def send_on(src, place, k, j, peer):
        return pltpu.make_async_remote_copy(
            src_ref=src,
            dst_ref=place,
            send_sem=c_send.at[k, j],
            recv_sem=c_recv.at[k, j],
            device_id=(half, row, peer),
            device_id_type=MESH,
        )

    def place_of(owner, k, part_of):
        start = behind(k) * chunk
        if part_of is None:
            return gens.at[owner, rows_of(start, chunk), :]
        return gens.at[owner, rows_of(start + part_of * cut, cut), :]

    def c_copy(k, j):
        owner, part_of, peer = (
            (col, None, side_a),
            (col, None, side_b),
            (side_a, 0, side_b),
            (side_b, 1, side_a),
        )[j]
        place = place_of(owner, k, part_of)
        return send_on(place, place, k, j, peer)

    def c_arrived(k, j):
        corner = n_col - 1 - col
        owner, part_of, peer = (
            (side_a, None, side_a),
            (side_b, None, side_b),
            (corner, 0, side_b),
            (corner, 1, side_a),
        )[j]
        place = place_of(owner, k, part_of)
        return send_on(place, place, k, j, peer)

    def start_z(k, carry):
        z_copy(k).start()
        return carry

    own_chunk = rows_of(row * chunk, chunk)
    gens[col, own_chunk, :] = gen_ref[own_chunk, :]
    for j in range(2):
        c_copy(0, j).start()
    lax.fori_loop(1, n_row, start_z, 0)

    x_place = pair.at[rows_of(half * rows, rows), :]
    x_copy = pltpu.make_async_remote_copy(
        src_ref=x_ref,
        dst_ref=x_place,
        send_sem=x_sem.at[0],
        recv_sem=x_sem.at[1],
        device_id=(other, row, col),
        device_id_type=MESH,
    )
    x_copy.start()
    pair[rows_of(half * rows, rows), :] = x_ref[...]

    has_low, has_high = flat > 0, flat < n_half * n_row - 1

    def edge_copy(j):
        return pltpu.make_async_remote_copy(
            src_ref=edge_ref.at[j],
            dst_ref=halo.at[1 - j],
            send_sem=e_send.at[j],
            recv_sem=e_recv.at[1 - j],
            device_id=device(flat - 1 + 2 * j),
            device_id_type=MESH,
        )

    for j, there in enumerate((has_low, has_high)):

        @pl.when(there)
        def _(j=j):
            edge_copy(j).start()

        @pl.when(jnp.logical_not(there))
        def _(j=j):
            halo[j] = jnp.zeros_like(halo[j])

    part[...] = jnp.zeros_like(part)
    weights[...] = jnp.zeros_like(weights)
    x_copy.wait_recv()

    def multiply(k):
        start = rows_of(behind(k) * chunk, chunk)
        wide = jnp.concatenate([gens[c, start, :] for c in range(n_col)], axis=1)
        product = lax.dot_general(
            pair[start, :], wide, (((0,), (0,)), ((), ())), preferred_element_type=F32
        )
        for c in range(n_col):
            part[c * panel : (c + 1) * panel, :] += product[:, c * panel : (c + 1) * panel]

    def finish(k):
        for j in range(2, 4):
            c_arrived(k, j).wait_recv()
        multiply(k)

    def pass_on(k):
        for j in range(2):
            c_arrived(k, j).wait_recv()
            c_copy(k, j + 2).start()

    def step(k, carry):
        z_arrived(k).wait_recv()
        for j in range(2):
            c_copy(k, j).start()
        pass_on(k - 1)

        @pl.when(k >= 2)
        def _():
            finish(k - 2)

        return carry

    lax.fori_loop(1, n_row, step, 0)
    pass_on(n_row - 1)
    finish(n_row - 2)
    finish(n_row - 1)

    def p_copy(k):
        return pltpu.make_async_remote_copy(
            src_ref=part.at[rows_of(ahead(k) * unit, unit), :],
            dst_ref=terms.at[k],
            send_sem=p_send.at[k],
            recv_sem=p_recv.at[k],
            device_id=(half, ahead(k), col),
            device_id_type=MESH,
        )

    def start_p(k, carry):
        p_copy(k).start()
        return carry

    lax.fori_loop(1, n_row, start_p, 0)
    own_unit = rows_of(row * unit, unit)

    def add_p(k, carry):
        p_copy(k).wait_recv()
        return carry + terms[k]

    share = lax.fori_loop(1, n_row, add_p, part[own_unit, :])
    held[own_unit, :] = share.astype(BF16).astype(held.dtype)

    def q_copy(k):
        place = held.at[own_unit, :]
        return pltpu.make_async_remote_copy(
            src_ref=place,
            dst_ref=place,
            send_sem=q_send.at[k],
            recv_sem=q_recv.at[k],
            device_id=(half, ahead(k), col),
            device_id_type=MESH,
        )

    def q_arrived(k):
        place = held.at[rows_of(behind(k) * unit, unit), :]
        return pltpu.make_async_remote_copy(
            src_ref=place,
            dst_ref=place,
            send_sem=q_send.at[k],
            recv_sem=q_recv.at[k],
            device_id=(half, behind(k), col),
            device_id_type=MESH,
        )

    def start_q(k, carry):
        q_copy(k).start()
        return carry

    def wait_q(k, carry):
        q_arrived(k).wait_recv()
        return carry

    lax.fori_loop(1, n_row, start_q, 0)
    lax.fori_loop(1, n_row, wait_q, 0)

    ranks = gen_ref.shape[1] // 2
    for c in range(n_col):
        turned = held[c * panel : (c + 1) * panel, :].astype(F32).T.astype(BF16)
        top = c * 2 * ranks
        weights[top : top + ranks, :panel] = turned[ranks:]
        weights[top + ranks : top + 2 * ranks, panel:] = turned[:ranks]

    tiles = h_send.shape[0]
    tile = rows // tiles

    def part_of(start):
        where = pl.ds(pl.multiple_of(start, tile), tile)
        wide = jnp.concatenate([gens[c, where, :] for c in range(n_col)], axis=1)
        return jnp.dot(wide, weights[...], preferred_element_type=F32).astype(BF16)

    def h_copy(t):
        return pltpu.make_async_remote_copy(
            src_ref=leaving.at[t],
            dst_ref=landed.at[t],
            send_sem=h_send.at[t],
            recv_sem=h_recv.at[t],
            device_id=(other, row, col),
            device_id_type=MESH,
        )

    def leave(t, carry):
        leaving[t] = part_of(other * rows + t * tile)
        h_copy(t).start()
        return carry

    lax.fori_loop(0, tiles, leave, 0)

    for j, there in enumerate((has_low, has_high)):

        @pl.when(there)
        def _(j=j):
            edge_copy(1 - j).wait_recv()

    for t in range(tiles):
        mine = part_of(half * rows + t * tile).astype(F32)
        h_copy(t).wait_recv()
        both = mine + landed[t].astype(F32)
        where = slice(t * tile, (t + 1) * tile)
        range_out[where, :] = (range_ref[where, :] + both[:, :panel]).astype(BF16)
        total_rows = rows_ref[where, :] + both[:, panel:]
        if t == 0:
            total_rows += halo[0].astype(F32)
        if t == tiles - 1:
            total_rows += halo[1].astype(F32)
        rows_out[where, :] = total_rows.astype(BF16)

    def sent(k, carry):
        z_copy(k).wait_send()
        p_copy(k).wait_send()
        q_copy(k).wait_send()
        return carry

    lax.fori_loop(1, n_row, sent, 0)

    def passed(k, carry):
        for j in range(4):
            c_copy(k, j).wait_send()
        return carry

    lax.fori_loop(0, n_row, passed, 0)

    def left(t, carry):
        h_copy(t).wait_send()
        return carry

    lax.fori_loop(0, tiles, left, 0)
    x_copy.wait_send()
    for j, there in enumerate((has_low, has_high)):

        @pl.when(there)
        def _(j=j):
            edge_copy(j).wait_send()


def shards(sizes, samples, couplings, coupling_cols, child_map, gen_left, gen_right):
    n_half, n_row, n_col = sizes
    rows, panel = samples.shape
    edge = HB * BS
    total = gen_left.shape[2]
    ranks = gen_left.shape[1]
    axes = ("half", "row")
    count = n_half * n_row
    forward = [(i, i + 1) for i in range(count - 1)]
    backward = [(target, source) for source, target in forward]
    low = lax.ppermute(samples[rows - edge :], axes, forward)
    high = lax.ppermute(samples[:edge], axes, backward)
    params = pltpu.CompilerParams(vmem_limit_bytes=VMEM_LIMIT)
    gens = pl.pallas_call(
        prepare_kernel,
        out_shape=jax.ShapeDtypeStruct((total, 2 * ranks), BF16),
        in_specs=[smem(), vmem(), vmem()],
        out_specs=vmem(),
        compiler_params=params,
        cost_estimate=pl.CostEstimate(flops=0, bytes_accessed=4 * 2**20, transcendentals=0),
        name="prepare",
    )(child_map, gen_left, gen_right)
    sparse_range, sparse_rows, edges = pl.pallas_call(
        sparse_kernel,
        out_shape=(
            jax.ShapeDtypeStruct((rows, panel), F32),
            jax.ShapeDtypeStruct((rows, panel), F32),
            jax.ShapeDtypeStruct((2, edge, panel), BF16),
        ),
        in_specs=[smem()] + [vmem()] * 4,
        out_specs=(vmem(), vmem(), vmem()),
        scratch_shapes=[
            pltpu.VMEM((rows + 2 * edge, panel), BF16),
            pltpu.VMEM((rows + 2 * edge, panel), F32),
        ],
        compiler_params=params,
        name="couple",
    )(coupling_cols, low, samples, high, couplings)
    unit = n_col * panel // n_row
    tiles = rows // edge
    dma = pltpu.SemaphoreType.DMA
    return pl.pallas_call(
        functools.partial(exchange_kernel, n_half, n_row, n_col),
        out_shape=(jax.ShapeDtypeStruct((rows, panel), BF16),) * 2,
        in_specs=[vmem()] * 5,
        out_specs=(vmem(), vmem()),
        scratch_shapes=[
            pltpu.VMEM((n_col, total, 2 * ranks), BF16),
            pltpu.VMEM((n_half * rows, panel), BF16),
            pltpu.VMEM((n_col * panel, 2 * ranks), F32),
            pltpu.VMEM((n_row, unit, 2 * ranks), F32),
            pltpu.VMEM((n_col * panel, 2 * ranks), BF16 if unit % 16 == 0 else F32),
            pltpu.VMEM((n_col * 2 * ranks, 2 * panel), BF16),
            pltpu.VMEM((tiles, rows // tiles, 2 * panel), BF16),
            pltpu.VMEM((tiles, rows // tiles, 2 * panel), BF16),
            pltpu.VMEM((2, edge, panel), BF16),
            dma((2,)),
            dma((n_row,)),
            dma((n_row,)),
            dma((n_row, 4)),
            dma((n_row, 4)),
            dma((n_row,)),
            dma((n_row,)),
            dma((n_row,)),
            dma((n_row,)),
            dma((tiles,)),
            dma((tiles,)),
            dma((2,)),
            dma((2,)),
        ],
        compiler_params=pltpu.CompilerParams(
            vmem_limit_bytes=VMEM_LIMIT, collective_id=0, has_side_effects=True
        ),
        name="exchange",
    )(gens, samples, sparse_range, sparse_rows, edges)


def solution(mesh):
    placed = (
        P(("half", "row"), "col"),
        P(("half", "row"), None, None),
        P(("half", "row"), None),
        P("half", "row", None),
        P("half", "col", "row"),
        P("half", "col", "row"),
    )
    sizes = tuple(mesh.shape[axis] for axis in ("half", "row", "col"))
    return jax.shard_map(
        functools.partial(shards, sizes),
        mesh=mesh,
        in_specs=placed,
        out_specs=(P(("half", "row"), "col"), P(("half", "row"), "col")),
        check_vma=False,
    )
```

```python
import functools

import jax
import jax.numpy as jnp
from jax import lax
from jax.experimental import pallas as pl
from jax.experimental.pallas import tpu as pltpu
from jax.sharding import PartitionSpec as P

BS = 64
NB = 8
HB = 8
MESH = pl.DeviceIdType.MESH
VMEM_LIMIT = 48 * 1024 * 1024
F32 = jnp.float32
BF16 = jnp.bfloat16


def vmem():
    return pl.BlockSpec(memory_space=pltpu.VMEM)


def smem():
    return pl.BlockSpec(memory_space=pltpu.SMEM)


def hbm():
    return pl.BlockSpec(memory_space=pltpu.HBM)


def prepare_kernel(
    map_any,
    left_any,
    right_any,
    cols_any,
    x_any,
    a_any,
    out_ref,
    range_ref,
    rows_ref,
    edge_ref,
    band_ref,
    map_ref,
    left_ref,
    right_ref,
    cols_ref,
    x_ref,
    a_ref,
    spread,
    padded,
    dense,
    sems,
):
    copies = [
        pltpu.make_async_copy(src, dst, sems.at[i])
        for i, (src, dst) in enumerate(
            (
                (map_any, map_ref),
                (left_any, left_ref),
                (right_any, right_ref),
                (cols_any, cols_ref),
                (x_any, x_ref),
                (a_any, a_ref),
            )
        )
    ]
    for copy in copies:
        copy.start()
    pairs = left_ref.shape[2] // (2 * BS)
    count = a_ref.shape[0]
    rows = x_ref.shape[0]
    halo = HB * BS
    first = (lax.axis_index("half") * lax.axis_size("row") + lax.axis_index("row")) * count
    spread[...] = jnp.zeros_like(spread)
    dense[...] = jnp.zeros_like(dense)
    padded[...] = jnp.zeros_like(padded)
    for copy in copies[:3]:
        copy.wait()

    def turn(i, carry):
        lanes = pl.ds(pl.multiple_of(i * 2 * BS, 2 * BS), 2 * BS)
        tile = jnp.concatenate([left_ref[0, :, lanes], right_ref[0, :, lanes]], axis=0).T
        for u in range(2):
            place = pl.multiple_of(map_ref[0, 0, 2 * i + u] * BS, BS)
            out_ref[pl.ds(place, BS), :] = tile[u * BS : (u + 1) * BS]
        return carry

    lax.fori_loop(0, pairs, turn, 0, unroll=4)
    for copy in copies[3:]:
        copy.wait()
    padded[halo : halo + rows] = x_ref[...]

    def step(b, carry):
        own = pl.ds(pl.multiple_of(b * BS, BS), BS)
        pieces = lax.dot_general(
            a_ref[b], x_ref[own, :], (((0,), (0,)), ((), ())), preferred_element_type=F32
        )
        at = [pl.multiple_of((cols_ref[b, t] - first + HB) * BS, BS) for t in range(NB)]
        picked = jnp.concatenate([padded[pl.ds(p, BS), :] for p in at], axis=0)
        range_ref[own, :] = jnp.dot(a_ref[b], picked, preferred_element_type=F32)
        for t in range(NB):
            spread[pl.ds(at[t], BS), :] += pieces[t * BS : (t + 1) * BS]
        return carry

    lax.fori_loop(0, count, step, 0, unroll=2)
    for side in range(2):
        for u in range(HB):
            b = u + side * (count - HB)
            turned = a_ref[b].astype(F32).T
            for t in range(NB):
                offset = cols_ref[b, t] - first + HB - side * (count + HB)
                inside = jnp.logical_and(offset >= 0, offset < HB)
                place = pl.multiple_of(jnp.where(inside, offset, HB) * BS, BS)
                dense[side, pl.ds(place, BS), u * BS : (u + 1) * BS] += turned[
                    t * BS : (t + 1) * BS
                ]
        band_ref[side] = dense[side, :halo].astype(BF16)
    rows_ref[...] = spread[halo : halo + rows]
    edge_ref[0] = spread[:halo].astype(BF16)
    edge_ref[1] = spread[halo + rows :].astype(BF16)


def exchange_kernel(
    n_half,
    n_row,
    n_col,
    gen_ref,
    x_ref,
    range_ref,
    rows_ref,
    edge_ref,
    band_ref,
    range_out,
    rows_out,
    gens,
    pair,
    part,
    terms,
    held,
    weights,
    leaving,
    landed,
    halo,
    wire,
    padded,
    x_sem,
    z_send,
    z_recv,
    c_send,
    c_recv,
    p_send,
    p_recv,
    q_send,
    q_recv,
    h_send,
    h_recv,
    e_send,
    e_recv,
    n_send,
    n_recv,
):
    half, row, col = lax.axis_index("half"), lax.axis_index("row"), lax.axis_index("col")
    rows, panel = x_ref.shape
    total = gen_ref.shape[0]
    chunk = total // n_row
    cut = chunk // 2
    unit = n_col * panel // n_row
    edge = HB * BS
    flat = half * n_row + row
    other = 1 - half
    side_a = col + 1 - 2 * lax.rem(col, 2)
    side_b = lax.rem(col + 2, n_col)

    def ahead(k):
        return lax.rem(row + k, n_row)

    def behind(k):
        return lax.rem(row + n_row - k, n_row)

    def device(index):
        return (index // n_row, lax.rem(index, n_row), col)

    seam_low = jnp.logical_and(half == 0, row == n_row - 1)
    seam_high = jnp.logical_and(half == 1, row == 0)

    barrier = pltpu.get_barrier_semaphore()

    def greet(k, carry):
        pl.semaphore_signal(
            barrier, inc=1, device_id=(half, ahead(k), col), device_id_type=MESH
        )
        return carry

    lax.fori_loop(1, n_row, greet, 0)
    for peer in ((other, row, col), (half, row, side_a), (half, row, side_b)):
        pl.semaphore_signal(barrier, inc=1, device_id=peer, device_id_type=MESH)

    @pl.when(seam_low)
    def _():
        pl.semaphore_signal(
            barrier, inc=1, device_id=(other, ahead(1), col), device_id_type=MESH
        )

    @pl.when(seam_high)
    def _():
        pl.semaphore_signal(
            barrier, inc=1, device_id=(other, behind(1), col), device_id_type=MESH
        )

    seams = jnp.where(jnp.logical_or(seam_low, seam_high), 1, 0)
    pl.semaphore_wait(barrier, n_row + 2 + seams)

    def rows_of(start, size):
        return pl.ds(pl.multiple_of(start, size), size)

    def z_copy(k):
        return pltpu.make_async_remote_copy(
            src_ref=gen_ref.at[rows_of(ahead(k) * chunk, chunk), :],
            dst_ref=gens.at[col, rows_of(row * chunk, chunk), :],
            send_sem=z_send.at[k],
            recv_sem=z_recv.at[k],
            device_id=(half, ahead(k), col),
            device_id_type=MESH,
        )

    def z_arrived(k):
        place = gens.at[col, rows_of(behind(k) * chunk, chunk), :]
        return pltpu.make_async_remote_copy(
            src_ref=place,
            dst_ref=place,
            send_sem=z_send.at[k],
            recv_sem=z_recv.at[k],
            device_id=(half, behind(k), col),
            device_id_type=MESH,
        )

    def send_on(src, place, k, j, peer):
        return pltpu.make_async_remote_copy(
            src_ref=src,
            dst_ref=place,
            send_sem=c_send.at[k, j],
            recv_sem=c_recv.at[k, j],
            device_id=(half, row, peer),
            device_id_type=MESH,
        )

    def place_of(owner, k, part_of):
        start = behind(k) * chunk
        if part_of is None:
            return gens.at[owner, rows_of(start, chunk), :]
        return gens.at[owner, rows_of(start + part_of * cut, cut), :]

    def c_copy(k, j):
        owner, part_of, peer = (
            (col, None, side_a),
            (col, None, side_b),
            (side_a, 0, side_b),
            (side_b, 1, side_a),
        )[j]
        place = place_of(owner, k, part_of)
        return send_on(place, place, k, j, peer)

    def c_arrived(k, j):
        corner = n_col - 1 - col
        owner, part_of, peer = (
            (side_a, None, side_a),
            (side_b, None, side_b),
            (corner, 0, side_b),
            (corner, 1, side_a),
        )[j]
        place = place_of(owner, k, part_of)
        return send_on(place, place, k, j, peer)

    def start_z(k, carry):
        z_copy(k).start()
        return carry

    own_chunk = rows_of(row * chunk, chunk)
    gens[col, own_chunk, :] = gen_ref[own_chunk, :]
    for j in range(2):
        c_copy(0, j).start()
    line = n_row == 4
    inner = jnp.logical_and(row > 0, row < n_row - 1)
    at_low = row == 0
    at_high = row == n_row - 1

    def order(i):
        if not line:
            return i
        ends = jnp.where(at_low, lax.rem(n_row - i, n_row), i)
        swapped = jnp.where(i == 2, 3, jnp.where(i == 3, 2, i))
        return jnp.where(jnp.logical_or(at_low, at_high), ends, swapped)

    def z_order(i):
        return n_row - order(i)

    if line:
        z_copy(z_order(1)).start()

        @pl.when(inner)
        def _():
            z_copy(z_order(2)).start()

    else:
        lax.fori_loop(1, n_row, start_z, 0)

    x_place = pair.at[rows_of(half * rows, rows), :]
    x_copy = pltpu.make_async_remote_copy(
        src_ref=x_ref,
        dst_ref=x_place,
        send_sem=x_sem.at[0],
        recv_sem=x_sem.at[1],
        device_id=(other, row, col),
        device_id_type=MESH,
    )
    x_copy.start()
    pair[rows_of(half * rows, rows), :] = x_ref[...]

    has_low, has_high = flat > 0, flat < n_half * n_row - 1

    def edge_copy(j):
        return pltpu.make_async_remote_copy(
            src_ref=edge_ref.at[j],
            dst_ref=halo.at[1 - j],
            send_sem=e_send.at[j],
            recv_sem=e_recv.at[1 - j],
            device_id=device(flat - 1 + 2 * j),
            device_id_type=MESH,
        )

    def near_copy(j):
        here = (0, rows - edge)[j]
        there = (edge, 0)[j]
        return pltpu.make_async_remote_copy(
            src_ref=x_ref.at[here : here + edge, :],
            dst_ref=padded.at[there : there + edge, :],
            send_sem=n_send.at[j],
            recv_sem=n_recv.at[1 - j],
            device_id=device(flat - 1 + 2 * j),
            device_id_type=MESH,
        )

    for j, there in enumerate((has_low, has_high)):

        @pl.when(jnp.logical_not(there))
        def _(j=j):
            at = (0, edge)[j]
            padded[at : at + edge] = jnp.zeros((edge, panel), BF16)
            halo[j] = jnp.zeros_like(halo[j])

    part[...] = jnp.zeros_like(part)
    weights[...] = jnp.zeros_like(weights)
    if line:
        z_copy(z_order(1)).wait_send()

        @pl.when(inner)
        def _():
            z_copy(z_order(2)).wait_send()
            z_copy(z_order(3)).start()

        @pl.when(jnp.logical_not(inner))
        def _():
            z_copy(z_order(2)).start()

    x_copy.wait_recv()

    def multiply(k):
        start = rows_of(behind(k) * chunk, chunk)
        wide = jnp.concatenate([gens[c, start, :] for c in range(n_col)], axis=1)
        product = lax.dot_general(
            pair[start, :], wide, (((0,), (0,)), ((), ())), preferred_element_type=F32
        )
        for c in range(n_col):
            part[c * panel : (c + 1) * panel, :] += product[:, c * panel : (c + 1) * panel]

    def finish(k):
        for j in range(2, 4):
            c_arrived(k, j).wait_recv()
        multiply(k)

    def pass_on(k):
        for j in range(2):
            c_arrived(k, j).wait_recv()
            c_copy(k, j + 2).start()

    def step(i, carry):
        k = order(i)
        z_arrived(k).wait_recv()
        for j in range(2):
            c_copy(k, j).start()
        if line:

            @pl.when(jnp.logical_and(i == 1, jnp.logical_not(inner)))
            def _():
                z_copy(z_order(2)).wait_send()
                z_copy(z_order(3)).start()

        pass_on(order(i - 1))

        @pl.when(i >= 2)
        def _():
            finish(order(i - 2))

        return carry

    lax.fori_loop(1, n_row, step, 0)
    for j, there in enumerate((has_low, has_high)):

        @pl.when(there)
        def _(j=j):
            near_copy(j).start()
            edge_copy(j).start()

    pass_on(order(n_row - 1))
    finish(order(n_row - 2))
    for j, there in enumerate((has_low, has_high)):

        @pl.when(there)
        def _(j=j):
            near_copy(1 - j).wait_recv()

    finish(order(n_row - 1))

    def p_copy(k):
        return pltpu.make_async_remote_copy(
            src_ref=wire.at[rows_of(ahead(k) * unit, unit), :],
            dst_ref=terms.at[k],
            send_sem=p_send.at[k],
            recv_sem=p_recv.at[k],
            device_id=(half, ahead(k), col),
            device_id_type=MESH,
        )

    def start_p(k, carry):
        p_copy(k).start()
        return carry

    wire[...] = part[...].astype(wire.dtype)
    lax.fori_loop(1, n_row, start_p, 0)
    own_unit = rows_of(row * unit, unit)

    def add_p(k, carry):
        p_copy(k).wait_recv()
        return carry + terms[k].astype(F32)

    share = lax.fori_loop(1, n_row, add_p, part[own_unit, :])
    held[own_unit, :] = share.astype(BF16).astype(held.dtype)

    def q_copy(k):
        place = held.at[own_unit, :]
        return pltpu.make_async_remote_copy(
            src_ref=place,
            dst_ref=place,
            send_sem=q_send.at[k],
            recv_sem=q_recv.at[k],
            device_id=(half, ahead(k), col),
            device_id_type=MESH,
        )

    def q_arrived(k):
        place = held.at[rows_of(behind(k) * unit, unit), :]
        return pltpu.make_async_remote_copy(
            src_ref=place,
            dst_ref=place,
            send_sem=q_send.at[k],
            recv_sem=q_recv.at[k],
            device_id=(half, behind(k), col),
            device_id_type=MESH,
        )

    def start_q(k, carry):
        q_copy(k).start()
        return carry

    def wait_q(k, carry):
        q_arrived(k).wait_recv()
        return carry

    lax.fori_loop(1, n_row, start_q, 0)
    lax.fori_loop(1, n_row, wait_q, 0)

    ranks = gen_ref.shape[1] // 2
    for c in range(n_col):
        turned = held[c * panel : (c + 1) * panel, :].astype(F32).T.astype(BF16)
        top = c * 2 * ranks
        weights[top : top + ranks, :panel] = turned[ranks:]
        weights[top + ranks : top + 2 * ranks, panel:] = turned[:ranks]

    tiles = h_send.shape[0]
    tile = rows // tiles

    def part_of(start):
        where = pl.ds(pl.multiple_of(start, tile), tile)
        wide = jnp.concatenate([gens[c, where, :] for c in range(n_col)], axis=1)
        return jnp.dot(wide, weights[...], preferred_element_type=F32).astype(BF16)

    def h_copy(t):
        return pltpu.make_async_remote_copy(
            src_ref=leaving.at[t],
            dst_ref=landed.at[t],
            send_sem=h_send.at[t],
            recv_sem=h_recv.at[t],
            device_id=(other, row, col),
            device_id_type=MESH,
        )

    def leave(t, carry):
        leaving[t] = part_of(other * rows + t * tile)
        h_copy(t).start()
        return carry

    lax.fori_loop(0, tiles, leave, 0)

    for j, there in enumerate((has_low, has_high)):

        @pl.when(there)
        def _(j=j):
            edge_copy(1 - j).wait_recv()

    for t in range(tiles):
        mine = part_of(half * rows + t * tile).astype(F32)
        h_copy(t).wait_recv()
        both = mine + landed[t].astype(F32)
        where = slice(t * tile, (t + 1) * tile)
        total_range = range_ref[where, :] + both[:, :panel]
        for side, at in enumerate((0, tiles - 1)):
            if t == at:
                total_range += lax.dot_general(
                    band_ref[side],
                    padded[side * edge : (side + 1) * edge, :],
                    (((0,), (0,)), ((), ())),
                    preferred_element_type=F32,
                )
        range_out[where, :] = total_range.astype(BF16)
        total_rows = rows_ref[where, :] + both[:, panel:]
        if t == 0:
            total_rows += halo[0].astype(F32)
        if t == tiles - 1:
            total_rows += halo[1].astype(F32)
        rows_out[where, :] = total_rows.astype(BF16)

    def sent(k, carry):
        if not line:
            z_copy(k).wait_send()
        p_copy(k).wait_send()
        q_copy(k).wait_send()
        return carry

    lax.fori_loop(1, n_row, sent, 0)

    def passed(k, carry):
        for j in range(4):
            c_copy(k, j).wait_send()
        return carry

    lax.fori_loop(0, n_row, passed, 0)

    def left(t, carry):
        h_copy(t).wait_send()
        return carry

    lax.fori_loop(0, tiles, left, 0)
    if line:
        z_copy(z_order(3)).wait_send()
    x_copy.wait_send()
    for j, there in enumerate((has_low, has_high)):

        @pl.when(there)
        def _(j=j):
            edge_copy(j).wait_send()
            near_copy(j).wait_send()


def shards(sizes, samples, couplings, coupling_cols, child_map, gen_left, gen_right):
    n_half, n_row, n_col = sizes
    rows, panel = samples.shape
    edge = HB * BS
    total = gen_left.shape[2]
    ranks = gen_left.shape[1]
    gens, sparse_range, sparse_rows, edges, band = pl.pallas_call(
        prepare_kernel,
        out_shape=(
            jax.ShapeDtypeStruct((total, 2 * ranks), BF16),
            jax.ShapeDtypeStruct((rows, panel), F32),
            jax.ShapeDtypeStruct((rows, panel), F32),
            jax.ShapeDtypeStruct((2, edge, panel), BF16),
            jax.ShapeDtypeStruct((2, edge, edge), BF16),
        ),
        in_specs=[hbm()] * 6,
        out_specs=(vmem(),) * 5,
        scratch_shapes=[
            pltpu.SMEM(child_map.shape, jnp.int32),
            pltpu.VMEM(gen_left.shape, BF16),
            pltpu.VMEM(gen_right.shape, BF16),
            pltpu.SMEM(coupling_cols.shape, jnp.int32),
            pltpu.VMEM(samples.shape, BF16),
            pltpu.VMEM(couplings.shape, BF16),
            pltpu.VMEM((rows + 2 * edge, panel), F32),
            pltpu.VMEM((rows + 2 * edge, panel), BF16),
            pltpu.VMEM((2, edge + BS, edge), F32),
            pltpu.SemaphoreType.DMA((6,)),
        ],
        compiler_params=pltpu.CompilerParams(vmem_limit_bytes=VMEM_LIMIT),
        name="prepare",
    )(child_map, gen_left, gen_right, coupling_cols, samples, couplings)
    unit = n_col * panel // n_row
    tiles = rows // edge
    wire_type = BF16 if unit % 16 == 0 else F32
    dma = pltpu.SemaphoreType.DMA
    return pl.pallas_call(
        functools.partial(exchange_kernel, n_half, n_row, n_col),
        out_shape=(jax.ShapeDtypeStruct((rows, panel), BF16),) * 2,
        in_specs=[vmem()] * 6,
        out_specs=(vmem(), vmem()),
        scratch_shapes=[
            pltpu.VMEM((n_col, total, 2 * ranks), BF16),
            pltpu.VMEM((n_half * rows, panel), BF16),
            pltpu.VMEM((n_col * panel, 2 * ranks), F32),
            pltpu.VMEM((n_row, unit, 2 * ranks), wire_type),
            pltpu.VMEM((n_col * panel, 2 * ranks), wire_type),
            pltpu.VMEM((n_col * 2 * ranks, 2 * panel), BF16),
            pltpu.VMEM((tiles, rows // tiles, 2 * panel), BF16),
            pltpu.VMEM((tiles, rows // tiles, 2 * panel), BF16),
            pltpu.VMEM((2, edge, panel), BF16),
            pltpu.VMEM((n_col * panel, 2 * ranks), wire_type),
            pltpu.VMEM((2 * edge, panel), BF16),
            dma((2,)),
            dma((n_row,)),
            dma((n_row,)),
            dma((n_row, 4)),
            dma((n_row, 4)),
            dma((n_row,)),
            dma((n_row,)),
            dma((n_row,)),
            dma((n_row,)),
            dma((tiles,)),
            dma((tiles,)),
            dma((2,)),
            dma((2,)),
            dma((2,)),
            dma((2,)),
        ],
        compiler_params=pltpu.CompilerParams(
            vmem_limit_bytes=VMEM_LIMIT, collective_id=0, has_side_effects=True
        ),
        name="exchange",
    )(gens, samples, sparse_range, sparse_rows, edges, band)


def solution(mesh):
    placed = (
        P(("half", "row"), "col"),
        P(("half", "row"), None, None),
        P(("half", "row"), None),
        P("half", "row", None),
        P("half", "col", "row"),
        P("half", "col", "row"),
    )
    sizes = tuple(mesh.shape[axis] for axis in ("half", "row", "col"))
    return jax.shard_map(
        functools.partial(shards, sizes),
        mesh=mesh,
        in_specs=placed,
        out_specs=(P(("half", "row"), "col"), P(("half", "row"), "col")),
        check_vma=False,
    )
```
